32 devices in a mesh: groups: 1, pairs: 4 (over z), chol: 4 (over y, x), walk: 2 (over core).
Axes of the slice: x: 2, y: 2, z: 4, core: 2. Of those that a mesh axis runs over, the one named last changes fastest.
Arguments:
- chol_vectors: bfloat16 [512, 768, 768], P(('groups', 'walk'), 'pairs', 'chol'), as said below
- trial_orbitals: float32 [768, 256], P('groups'), as said below
- walkers: float32 [16, 768, 256], P(('groups', 'pairs', 'chol'), None, 'walk'), as said below
- field_noise: float32 [1, 16, 512], P('groups', None, 'walk'), may hold values from -6 to 6
Outputs:
- propagated: float32 [16, 768, 256], P(('groups', 'pairs', 'chol'), None, 'walk')
- force_bias: float32 [1, 16, 512], P('groups', None, 'walk')
The draws below stay inside these ranges and needn't reach their ends.
Inputs may be any that keep to these rules, and one draw needn't show every extreme that they name: chol_vectors[g, p, q] = chol_vectors[g, q, p] for every g. The columns of trial_orbitals are linearly independent. `walkers`: every walker's intersection with trial_orbitals is far from singular.
All inputs are finite; a program needn't handle non-finite values.
Results may differ from the reference program's by a relative error of at most 0.0029.
Values may be sent and summed in bfloat16 or wider, within the bound.
A program may use at most 64 MiB of HBM per device.

```python
import math
import jax
import jax.numpy as jnp
from jax import lax

ORBITALS = 768
ELECTRONS = 256
WINDOW = 512
STEPS = 1
TERMS = 6
WALKERS = 16


def draw_chol_vectors(key, part):
    spread = 0.7 / (0.05 * math.sqrt(WINDOW * ORBITALS))
    base = jax.random.truncated_normal(key, -4.0, 4.0, (WINDOW, ORBITALS, ORBITALS), jnp.float32)
    return ((base + jnp.swapaxes(base, 1, 2)) * (spread / math.sqrt(2.0))).astype(jnp.bfloat16)


def draw_trial_orbitals(key, part):
    return jax.random.truncated_normal(jax.random.fold_in(key, 11), -5.0, 5.0, (ORBITALS, ELECTRONS), jnp.float32)


def draw_walkers(key, part):
    trial_base = draw_trial_orbitals(key, part)
    offsets = jax.random.truncated_normal(jax.random.fold_in(key, 12), -4.0, 4.0, (WALKERS, ORBITALS, ELECTRONS), jnp.float32)
    return 1.5 * (trial_base[None, :, :] + offsets)


def levels(own_key, shape, shards, least, high):
    loudness = 1.0
    for dim, parts in shards:
        steps = jax.random.uniform(jax.random.fold_in(jax.random.fold_in(own_key, 6), dim), (parts,), jnp.float32, least / len(shards), high / len(shards))
        loudness = loudness * jnp.repeat(jnp.exp(steps), shape[dim] // parts).reshape((-1,) + (1,) * (len(shape) - 1 - dim))
    return loudness


def gaussian(key, dims, scale, bound, split=(), kind=jnp.bfloat16):
    values = scale * jax.random.normal(key, dims, jnp.float32)
    if split:
        values = values * levels(key, dims, split, -0.22, 0.18)
    return jnp.clip(values, -bound, bound).astype(kind)


def setup_inputs(seed: int = 0, part: int = 0) -> dict:
    key_of = jax.random.split(jax.random.key(seed), 5)
    part_splits = jax.random.split(jax.random.fold_in(key_of[4], part), 5)
    chol_vectors = draw_chol_vectors(jax.random.fold_in(jax.random.fold_in(key_of[4], part), 71), part)
    trial_orbitals = draw_trial_orbitals(jax.random.fold_in(jax.random.fold_in(key_of[4], part), 71), part)
    walkers = draw_walkers(jax.random.fold_in(jax.random.fold_in(key_of[4], part), 71), part)
    field_noise = gaussian(part_splits[3], (STEPS, WALKERS, WINDOW), 1.0, 6.0, ((2, 2),), jnp.float32)
    return {"chol_vectors": chol_vectors, "trial_orbitals": trial_orbitals, "walkers": walkers, "field_noise": field_noise}


root_step = 0.05
highest = lax.Precision.HIGHEST

def solve_normal(factor, right_side):
    middle = lax.linalg.triangular_solve(factor, right_side, left_side=True, lower=True)
    return lax.linalg.triangular_solve(factor, middle, left_side=True, lower=True, transpose_a=True)

def green_matrix(walker, trial_orbitals):
    intersection = jnp.dot(trial_orbitals.T, walker, precision=highest)
    normal = jnp.dot(intersection.T, intersection, precision=highest)
    factor = jnp.linalg.cholesky(normal)
    rotated = jnp.dot(intersection.T, trial_orbitals.T, precision=highest)
    solved = solve_normal(factor, rotated)
    return jnp.dot(walker, solved, precision=highest).astype(jnp.bfloat16)

def propagate(matrix, walker):
    running_term = walker
    running_sum = walker
    for degree in range(1, TERMS):
        running_term = -(root_step / degree) * jnp.dot(matrix, running_term, precision=highest)
        running_sum = running_sum + running_term
    return running_sum

def reference(chol_vectors, trial_orbitals, walkers, field_noise):
    flat_vectors = chol_vectors.reshape(WINDOW, ORBITALS * ORBITALS)
    block_size = math.gcd(WINDOW, 64)
    block_count = WINDOW // block_size
    propagated = walkers
    bias_steps = []
    for step_index in range(STEPS):
        greens = lax.map(lambda walker: green_matrix(walker, trial_orbitals), propagated)
        greens_flat = greens.reshape(WALKERS, ORBITALS * ORBITALS)
        force_bias = lax.dot_general(greens_flat.astype(jnp.float32), flat_vectors.astype(jnp.float32), (((1,), (1,)), ((), ())), preferred_element_type=jnp.float32)
        bias_steps.append(force_bias)
        shifted = field_noise[step_index] + root_step * force_bias

        def add_block(running, block_index):
            start_index = (block_index * block_size).astype(jnp.int32)
            chosen = lax.dynamic_slice_in_dim(flat_vectors, start_index, block_size, 0).astype(jnp.float32)
            weights = lax.dynamic_slice_in_dim(shifted, start_index, block_size, 1)
            return (running + jnp.dot(weights, chosen, precision=highest), None)
        potential = lax.scan(add_block, jnp.zeros((WALKERS, ORBITALS * ORBITALS), jnp.float32), jnp.arange(block_count, dtype=jnp.int32))[0]
        propagated = lax.map(lambda packed: propagate(packed[0].reshape(ORBITALS, ORBITALS), packed[1]), (potential, propagated))
    return (propagated, jnp.stack(bias_steps))
```

```python
import functools

import jax
import jax.numpy as jnp
from jax import lax
from jax.experimental import pallas as pl
from jax.experimental.pallas import tpu as pltpu
from jax.sharding import PartitionSpec as P

TERMS = 6


root_step = 0.05
highest = lax.Precision.HIGHEST


def swapped(value, axis, apart):
    mask = 2**apart
    pairs = [(source, source ^ mask) for source in range(lax.axis_size(axis))]
    return lax.ppermute(value, axis, pairs)


def solve_normal(factor, right_side):
    middle = lax.linalg.triangular_solve(factor, right_side, left_side=True, lower=True)
    return lax.linalg.triangular_solve(factor, middle, left_side=True, lower=True, transpose_a=True)


def green_blocks(walker_full, trial_orbitals, trial_part, row_groups, col_groups):
    owner_walkers, orbital_count, electron_count = walker_full.shape
    intersection = jnp.einsum("nm,wnk->wmk", trial_orbitals, walker_full, precision=highest)
    normal = jnp.einsum("wmk,wml->wkl", intersection, intersection, precision=highest)
    factor = jnp.linalg.cholesky(normal)
    rotated = jnp.einsum("wmk,cbm->wkcb", intersection, trial_part, precision=highest)
    chosen_cols = rotated.shape[2] * rotated.shape[3]
    solved = solve_normal(factor, rotated.reshape(owner_walkers, electron_count, chosen_cols))
    slab_rows = orbital_count // row_groups
    block_cols = chosen_cols // col_groups
    shaped = solved.reshape(owner_walkers, electron_count, col_groups, block_cols)
    walker_rows = walker_full.reshape(owner_walkers, row_groups, slab_rows, electron_count)
    blocks = jnp.einsum("wiak,wkcb->icwab", walker_rows, shaped, precision=highest)
    return blocks.astype(jnp.bfloat16).reshape(
        row_groups * col_groups, owner_walkers, slab_rows * block_cols
    )


def plain_shards(chol_vectors, trial_orbitals, walkers, field_noise):
    held_vectors, slab_rows, slab_cols = chol_vectors.shape
    owner_walkers = walkers.shape[0]
    orbital_count = walkers.shape[1]
    electron_count = trial_orbitals.shape[1]
    row_groups = lax.axis_size("pairs")
    col_groups = lax.axis_size("chol")
    core_count = lax.axis_size("walk")
    core_index = lax.axis_index("walk")
    core_cols = slab_cols // core_count
    owner_count = row_groups * col_groups
    walker_total = owner_count * owner_walkers
    flat_vectors = chol_vectors.reshape(held_vectors, slab_rows * slab_cols)
    trial_split = trial_orbitals.reshape(col_groups, core_count, core_cols, electron_count)
    trial_part = lax.dynamic_index_in_dim(trial_split, core_index, 1, keepdims=False)
    walker_full = lax.all_gather(walkers, "walk", axis=2, tiled=True)
    outgoing = green_blocks(walker_full, trial_orbitals, trial_part, row_groups, col_groups)
    sectioned = outgoing.reshape(row_groups, col_groups, owner_walkers, slab_rows * core_cols)
    arrived = lax.all_to_all(
        lax.all_to_all(sectioned, "pairs", split_axis=0, concat_axis=0, tiled=True),
        "chol",
        split_axis=1,
        concat_axis=1,
        tiled=True,
    )
    arrived = arrived.reshape(walker_total, slab_rows, core_cols)
    partial_bias = jnp.einsum(
        "wab,gab->wg",
        lax.all_gather(arrived, "walk", axis=2, tiled=True),
        chol_vectors,
        preferred_element_type=jnp.float32,
    )
    force_bias = lax.psum(partial_bias, ("pairs", "chol"))
    bias_steps = [force_bias]
    shifted = field_noise[0] + root_step * force_bias
    shifted_high = lax.optimization_barrier(shifted.astype(jnp.bfloat16))
    shifted_low = (shifted - shifted_high.astype(jnp.float32)).astype(jnp.bfloat16)
    stacked = jnp.stack([shifted_high, shifted_low])
    both_parts = lax.dot_general(
        stacked, flat_vectors, (((2,), (0,)), ((), ())), preferred_element_type=jnp.float32
    )
    potential = both_parts[0] + both_parts[1]
    blocks_out = potential.reshape(owner_count, owner_walkers, slab_rows * slab_cols)
    received = lax.all_to_all(
        blocks_out, ("pairs", "chol"), split_axis=0, concat_axis=0, tiled=True
    )
    partner = swapped(received, "walk", 0)
    summed = (received + partner).reshape(
        row_groups, col_groups, owner_walkers, slab_rows, core_count, core_cols
    )
    matrix = jnp.transpose(summed, (2, 0, 3, 1, 4, 5)).reshape(
        owner_walkers, orbital_count, orbital_count
    )
    running_term = walkers
    running_sum = walkers
    for degree in range(1, TERMS):
        running_term = -(root_step / degree) * jnp.einsum(
            "wpq,wqm->wpm", matrix, running_term, precision=highest
        )
        running_sum = running_sum + running_term
    return (running_sum, jnp.stack(bias_steps))


PANEL = 32
TILE = 16
MIB = 2**20


def exact_dot(left, right, left_dim, right_dim):
    return lax.dot_general(
        left,
        right,
        (((left_dim,), (right_dim,)), ((), ())),
        precision=highest,
        preferred_element_type=jnp.float32,
    )


def fast_dot(left, right, left_dim, right_dim):
    return lax.dot_general(
        left, right, (((left_dim,), (right_dim,)), ((), ())), preferred_element_type=jnp.float32
    )


def green_kernel(row_groups, col_groups, walker_ref, trial_ref, out_ref, work):
    orbitals, electrons = walker_ref.shape
    core = lax.axis_index("walk")
    cores = lax.axis_size("walk")
    slab_rows = orbitals // row_groups
    slab_cols = orbitals // col_groups
    core_rows = slab_rows // cores
    half = core_rows // 2
    intersection = exact_dot(trial_ref[...], walker_ref[...], 0, 0)
    work[...] = exact_dot(intersection, intersection, 0, 0)
    lanes = lax.broadcasted_iota(jnp.int32, (PANEL, electrons), 1)
    rows = lax.broadcasted_iota(jnp.int32, (PANEL, electrons), 0)
    wide = lax.broadcasted_iota(jnp.int32, (electrons, electrons), 1)
    for start in range(0, electrons, PANEL):
        panel = work[start : start + PANEL, :]
        signed = jnp.where(lanes < start, -panel, panel)
        for step in range(PANEL):
            lane = start + step
            pivot_col = panel[:, lane : lane + 1]
            pivot = panel[step : step + 1, lane : lane + 1]
            scaled = jnp.where(lanes[:1] == lane, 1.0, panel[step : step + 1, :]) * (1.0 / pivot)
            cleared = jnp.where(lanes == lane, 0.0, panel) - pivot_col * scaled
            panel = jnp.where(rows == step, scaled, cleared)
        update = exact_dot(signed, panel, 0, 0)
        inside = (wide >= start) & (wide < start + PANEL)
        work[...] = jnp.where(inside, 0.0, work[...]) - update
        work[start : start + PANEL, :] = panel
    inverse = exact_dot(work[...], intersection, 1, 1)
    identity = jnp.where(
        lax.broadcasted_iota(jnp.int32, (electrons, electrons), 0) == wide, 1.0, 0.0
    )
    rest = identity - exact_dot(intersection, inverse, 1, 0)
    inverse = inverse + exact_dot(inverse, rest, 1, 0)
    chosen = jnp.concatenate(
        [
            walker_ref[pl.ds(pl.multiple_of(row * slab_rows + core * core_rows, 8), core_rows), :]
            for row in range(row_groups)
        ],
        axis=0,
    )
    left = exact_dot(chosen, inverse, 1, 0)
    for col in range(col_groups):
        block = exact_dot(left, trial_ref[col * slab_cols : (col + 1) * slab_cols, :], 1, 1)
        for row in range(row_groups):
            top = block[row * core_rows : row * core_rows + half]
            low = block[row * core_rows + half : (row + 1) * core_rows]
            out_ref[row * col_groups + col] = jnp.concatenate([top, low], axis=1).astype(jnp.bfloat16)


def walk_kernel(
    row_groups,
    col_groups,
    green_ref,
    vectors_ref,
    walker_ref,
    noise_ref,
    out_ref,
    bias_ref,
    held,
    greens,
    tiles,
    traces,
    first_sums,
    second_sums,
    spread,
    partner,
    own,
    ready,
    arrived,
    matrix,
    load_sem,
    green_send,
    green_recv,
    pass_send,
    pass_recv,
    first_send,
    first_recv,
    second_send,
    second_recv,
    partner_send,
    partner_recv,
    out_send,
    out_recv,
    hand_send,
    hand_recv,
):
    owners = row_groups * col_groups
    window, slab_rows, slab_cols = held.shape
    half = green_ref.shape[1]
    pieces = half // TILE
    blocks = slab_rows // TILE
    pair = lax.axis_index("pairs")
    place = lax.axis_index("chol")
    core = lax.axis_index("walk")
    me = pair * col_groups + place
    other = {"walk": 1 - core}

    def chip(index):
        return {"pairs": index // col_groups, "chol": index % col_groups}

    def to(shift):
        return lax.rem(me + shift, owners)

    def source(shift):
        return lax.rem(me + owners - shift, owners)

    def remote(src, dst, send, recv, target):
        return pltpu.make_async_remote_copy(
            src_ref=src,
            dst_ref=dst,
            send_sem=send,
            recv_sem=recv,
            device_id=target,
            device_id_type=pl.DeviceIdType.MESH,
        )

    parts = load_sem.shape[0]
    depth = window // parts
    loads = [
        pltpu.make_async_copy(
            vectors_ref.at[pl.ds(index * depth, depth)],
            held.at[pl.ds(index * depth, depth)],
            load_sem.at[index],
        )
        for index in range(parts)
    ]
    barrier = pltpu.get_barrier_semaphore()
    for shift in range(1, owners):
        pl.semaphore_signal(barrier, inc=1, device_id=chip(to(shift)), device_id_type=pl.DeviceIdType.MESH)
    pl.semaphore_signal(barrier, inc=1, device_id=other, device_id_type=pl.DeviceIdType.MESH)
    pl.semaphore_wait(barrier, owners)

    def green_copy(shift, slot):
        return remote(
            green_ref.at[to(shift)], greens.at[core, slot], green_send.at[shift],
            green_recv.at[shift], chip(to(shift)),
        )

    def pass_copy(shift, side):
        slot = source(shift)
        return remote(
            greens.at[side, slot], greens.at[side, slot], pass_send.at[shift], pass_recv.at[shift], other
        )

    for shift in range(1, owners):
        green_copy(shift, me).start()
    for load in loads:
        load.start()
    greens[core, me] = green_ref[me]
    pass_copy(0, core).start()
    for shift in range(1, owners):
        green_copy(shift, source(shift)).wait_recv()
        pass_copy(shift, core).start()
    for shift in range(1, owners):
        green_copy(shift, me).wait_send()
    for shift in range(owners):
        pass_copy(shift, 1 - core).wait_recv()
    for shift in range(owners):
        pass_copy(shift, core).wait_send()
    width = 2 * slab_cols
    for side in range(2):
        for piece in range(pieces):
            both = greens[side, :, piece * TILE : (piece + 1) * TILE, :].reshape(owners * TILE, width)
            tiles[side * 2 * pieces + piece] = both[:, :slab_cols]
            turned = pltpu.roll(both.astype(jnp.float32), slab_cols, 1)
            tiles[side * 2 * pieces + pieces + piece] = turned[:, :slab_cols].astype(jnp.bfloat16)
    for load in loads:
        load.wait()

    batch = min(window, 32)
    same = lax.rem(lax.broadcasted_iota(jnp.int32, (TILE, owners * TILE), 1), TILE) == (
        lax.broadcasted_iota(jnp.int32, (TILE, owners * TILE), 0)
    )

    @pl.loop(0, window // batch)
    def _(index):
        begin = pl.multiple_of(index * batch, batch)
        total = jnp.zeros((batch * TILE, owners * TILE), jnp.float32)
        for block in range(blocks):
            left = held[pl.ds(begin, batch), block * TILE : (block + 1) * TILE, :]
            total += fast_dot(left.reshape(batch * TILE, slab_cols), tiles[block], 1, 1)
        kept = jnp.where(same[None], total.reshape(batch, TILE, owners * TILE), 0.0)
        traces[pl.ds(begin, batch), :] = jnp.sum(kept, axis=1)

    walker_row = lax.broadcasted_iota(jnp.int32, (owners, owners * TILE), 0)
    column = lax.broadcasted_iota(jnp.int32, (owners, owners * TILE), 1)
    picker = jnp.where(walker_row == column // TILE, 1.0, 0.0)
    first_sums[place] = exact_dot(picker, traces[...], 1, 1)

    def first_copy(shift, slot):
        target = lax.rem(place + shift, col_groups)
        return remote(
            first_sums.at[slot], first_sums.at[slot], first_send.at[shift], first_recv.at[shift], {"chol": target}
        )

    def second_copy(shift, slot):
        target = lax.rem(pair + shift, row_groups)
        return remote(
            second_sums.at[slot], second_sums.at[slot], second_send.at[shift], second_recv.at[shift], {"pairs": target}
        )

    for shift in range(1, col_groups):
        first_copy(shift, place).start()
    for shift in range(1, col_groups):
        first_copy(shift, lax.rem(place + col_groups - shift, col_groups)).wait_recv()
    summed = first_sums[0]
    for slot in range(1, col_groups):
        summed = summed + first_sums[slot]
    second_sums[pair] = summed
    for shift in range(1, row_groups):
        second_copy(shift, pair).start()
    for shift in range(1, row_groups):
        second_copy(shift, lax.rem(pair + row_groups - shift, row_groups)).wait_recv()
    bias = second_sums[0]
    for slot in range(1, row_groups):
        bias = bias + second_sums[slot]
    bias_ref[0] = bias
    for shift in range(1, col_groups):
        first_copy(shift, place).wait_send()
    for shift in range(1, row_groups):
        second_copy(shift, pair).wait_send()

    shifted = (noise_ref[0] + root_step * bias).astype(jnp.bfloat16)
    tall = (owners * TILE, owners)
    repeat = jnp.where(
        lax.broadcasted_iota(jnp.int32, tall, 0) // TILE == lax.broadcasted_iota(jnp.int32, tall, 1), 1.0, 0.0
    ).astype(jnp.bfloat16)
    repeated = fast_dot(repeat, shifted, 1, 0).astype(jnp.bfloat16)
    group = 16
    spans = window // group
    square = (owners * TILE, group * TILE)
    diagonal = lax.rem(lax.broadcasted_iota(jnp.int32, square, 0), TILE) == lax.rem(
        lax.broadcasted_iota(jnp.int32, square, 1), TILE
    )
    for span in range(spans):
        shape = (window, group * TILE)
        opened = jnp.where(
            lax.broadcasted_iota(jnp.int32, shape, 0)
            == span * group + lax.broadcasted_iota(jnp.int32, shape, 1) // TILE,
            1.0,
            0.0,
        ).astype(jnp.bfloat16)
        wide = fast_dot(repeated, opened, 1, 0)
        spread[span] = jnp.where(diagonal, wide, 0.0).astype(jnp.bfloat16)

    def potential(block):
        row = pl.multiple_of(block * TILE, TILE)
        total = jnp.zeros((owners * TILE, slab_cols), jnp.float32)
        for span in range(spans):
            right = held[span * group : (span + 1) * group, pl.ds(row, TILE), :]
            total += fast_dot(spread[span], right.reshape(group * TILE, slab_cols), 1, 0)
        return total

    def packed(side, piece):
        first = side * 2 * pieces + piece
        both = jnp.concatenate([potential(first), potential(first + pieces)], axis=1)
        return both.reshape(owners, TILE, width)

    def partner_copy(piece):
        return remote(
            own.at[piece], partner.at[piece], partner_send.at[piece], partner_recv.at[piece], other
        )

    def out_copy(piece, shift, slot):
        span = pl.ds(piece * TILE, TILE)
        return remote(
            ready.at[to(shift), span], arrived.at[core, slot, span], out_send.at[piece, shift],
            out_recv.at[piece, shift], chip(to(shift)),
        )

    def hand_copy(shift, side):
        slot = source(shift)
        return remote(
            arrived.at[side, slot], arrived.at[side, slot], hand_send.at[shift], hand_recv.at[shift], other
        )

    for piece in range(pieces):
        own[piece] = packed(1 - core, piece)
        partner_copy(piece).start()
    for piece in range(pieces):
        mine = packed(core, piece)
        partner_copy(piece).wait_recv()
        ready[:, piece * TILE : (piece + 1) * TILE, :] = (mine + partner[piece]).astype(jnp.bfloat16)
        for shift in range(1, owners):
            out_copy(piece, shift, me).start()
    arrived[core, me] = ready[me]
    hand_copy(0, core).start()
    for shift in range(1, owners):
        for piece in range(pieces):
            out_copy(piece, shift, source(shift)).wait_recv()
        hand_copy(shift, core).start()
    for piece in range(pieces):
        partner_copy(piece).wait_send()
        for shift in range(1, owners):
            out_copy(piece, shift, me).wait_send()
    for shift in range(owners):
        hand_copy(shift, 1 - core).wait_recv()
    for shift in range(owners):
        hand_copy(shift, core).wait_send()
    for slot in range(owners):
        for side in range(2):
            base = (slot // col_groups) * slab_rows + side * 2 * half
            both = arrived[side, slot]
            matrix[slot % col_groups, base : base + half, :] = both[:, :slab_cols]
            turned = pltpu.roll(both.astype(jnp.float32), slab_cols, 1)
            matrix[slot % col_groups, base + half : base + 2 * half, :] = turned[:, :slab_cols].astype(jnp.bfloat16)

    term = walker_ref[0]
    out_ref[0] = term
    share = term.shape[1]
    for degree in range(1, TERMS):
        high = term.astype(jnp.bfloat16)
        low = (term - high.astype(jnp.float32)).astype(jnp.bfloat16)
        sides = jnp.concatenate([high, low], axis=1)
        total = jnp.zeros((term.shape[0], 2 * share), jnp.float32)
        for col in range(col_groups):
            total += fast_dot(matrix[col], sides[col * slab_cols : (col + 1) * slab_cols], 1, 0)
        term = -(root_step / degree) * (total[:, :share] + total[:, share:])
        out_ref[0] = out_ref[0] + term


def fits(chol_vectors, trial_orbitals, walkers):
    window, slab_rows, slab_cols = chol_vectors.shape
    electrons = trial_orbitals.shape[1]
    owners = lax.axis_size("pairs") * lax.axis_size("chol")
    return (
        lax.axis_size("walk") == 2
        and walkers.shape[0] == 1
        and walkers.shape[1] == trial_orbitals.shape[0]
        and slab_rows % (4 * TILE) == 0
        and (2 * slab_cols) % 128 == 0
        and window % 128 == 0
        and electrons % 256 == 0
        and owners <= 16
        and owners % 8 == 0
        and window * slab_rows * -(-slab_cols // 128) * 256 <= 28 * MIB
    )


def shards(chol_vectors, trial_orbitals, walkers, field_noise):
    if field_noise.shape[0] != 1 or not fits(chol_vectors, trial_orbitals, walkers):
        return plain_shards(chol_vectors, trial_orbitals, walkers, field_noise)
    row_groups = lax.axis_size("pairs")
    col_groups = lax.axis_size("chol")
    owners = row_groups * col_groups
    window, slab_rows, slab_cols = chol_vectors.shape
    orbitals, electrons = trial_orbitals.shape
    half = slab_rows // 4
    width = 2 * slab_cols
    pieces = half // TILE
    blocks = slab_rows // TILE
    walker_full = lax.all_gather(walkers[0], "walk", axis=1, tiled=True)
    in_vmem = pl.BlockSpec(memory_space=pltpu.VMEM)
    greens = pl.pallas_call(
        functools.partial(green_kernel, row_groups, col_groups),
        out_shape=jax.ShapeDtypeStruct((owners, half, width), jnp.bfloat16),
        in_specs=[in_vmem, in_vmem],
        out_specs=in_vmem,
        scratch_shapes=[pltpu.VMEM((electrons, electrons), jnp.float32)],
        compiler_params=pltpu.CompilerParams(vmem_limit_bytes=32 * MIB),
    )(walker_full, trial_orbitals)
    dma = pltpu.SemaphoreType.DMA
    propagated, bias = pl.pallas_call(
        functools.partial(walk_kernel, row_groups, col_groups),
        out_shape=(
            jax.ShapeDtypeStruct(walkers.shape, jnp.float32),
            jax.ShapeDtypeStruct(field_noise.shape, jnp.float32),
        ),
        in_specs=[in_vmem, pl.BlockSpec(memory_space=pl.ANY), in_vmem, in_vmem],
        out_specs=(in_vmem, in_vmem),
        scratch_shapes=[
            pltpu.VMEM(chol_vectors.shape, jnp.bfloat16),
            pltpu.VMEM((2, owners, half, width), jnp.bfloat16),
            pltpu.VMEM((blocks, owners * TILE, slab_cols), jnp.bfloat16),
            pltpu.VMEM((window, owners * TILE), jnp.float32),
            pltpu.VMEM((col_groups, owners, window), jnp.float32),
            pltpu.VMEM((row_groups, owners, window), jnp.float32),
            pltpu.VMEM((window // 16, owners * TILE, 16 * TILE), jnp.bfloat16),
            pltpu.VMEM((pieces, owners, TILE, width), jnp.float32),
            pltpu.VMEM((pieces, owners, TILE, width), jnp.float32),
            pltpu.VMEM((owners, half, width), jnp.bfloat16),
            pltpu.VMEM((2, owners, half, width), jnp.bfloat16),
            pltpu.VMEM((col_groups, orbitals, slab_cols), jnp.bfloat16),
            dma((4,)),
            dma((owners,)),
            dma((owners,)),
            dma((owners,)),
            dma((owners,)),
            dma((col_groups,)),
            dma((col_groups,)),
            dma((row_groups,)),
            dma((row_groups,)),
            dma((pieces,)),
            dma((pieces,)),
            dma((pieces, owners)),
            dma((pieces, owners)),
            dma((owners,)),
            dma((owners,)),
        ],
        compiler_params=pltpu.CompilerParams(
            collective_id=0, has_side_effects=True, vmem_limit_bytes=56 * MIB
        ),
    )(greens, chol_vectors, walkers, field_noise)
    return (propagated, bias)


def solution(mesh):
    placed = (
        P(("groups", "walk"), "pairs", "chol"),
        P("groups", None),
        P(("groups", "pairs", "chol"), None, "walk"),
        P("groups", None, "walk"),
    )
    return jax.shard_map(
        shards,
        mesh=mesh,
        in_specs=placed,
        out_specs=(P(("groups", "pairs", "chol"), None, "walk"), P("groups", None, "walk")),
        check_vma=False,
    )
```

```python
import functools

import jax
import jax.numpy as jnp
from jax import lax
from jax.experimental import pallas as pl
from jax.experimental.pallas import tpu as pltpu
from jax.sharding import PartitionSpec as P

TERMS = 6


root_step = 0.05
highest = lax.Precision.HIGHEST


def swapped(value, axis, apart):
    mask = 2**apart
    pairs = [(source, source ^ mask) for source in range(lax.axis_size(axis))]
    return lax.ppermute(value, axis, pairs)


def solve_normal(factor, right_side):
    middle = lax.linalg.triangular_solve(factor, right_side, left_side=True, lower=True)
    return lax.linalg.triangular_solve(factor, middle, left_side=True, lower=True, transpose_a=True)


def green_blocks(walker_full, trial_orbitals, trial_part, row_groups, col_groups):
    owner_walkers, orbital_count, electron_count = walker_full.shape
    intersection = jnp.einsum("nm,wnk->wmk", trial_orbitals, walker_full, precision=highest)
    normal = jnp.einsum("wmk,wml->wkl", intersection, intersection, precision=highest)
    factor = jnp.linalg.cholesky(normal)
    rotated = jnp.einsum("wmk,cbm->wkcb", intersection, trial_part, precision=highest)
    chosen_cols = rotated.shape[2] * rotated.shape[3]
    solved = solve_normal(factor, rotated.reshape(owner_walkers, electron_count, chosen_cols))
    slab_rows = orbital_count // row_groups
    block_cols = chosen_cols // col_groups
    shaped = solved.reshape(owner_walkers, electron_count, col_groups, block_cols)
    walker_rows = walker_full.reshape(owner_walkers, row_groups, slab_rows, electron_count)
    blocks = jnp.einsum("wiak,wkcb->icwab", walker_rows, shaped, precision=highest)
    return blocks.astype(jnp.bfloat16).reshape(
        row_groups * col_groups, owner_walkers, slab_rows * block_cols
    )


def plain_shards(chol_vectors, trial_orbitals, walkers, field_noise):
    held_vectors, slab_rows, slab_cols = chol_vectors.shape
    owner_walkers = walkers.shape[0]
    orbital_count = walkers.shape[1]
    electron_count = trial_orbitals.shape[1]
    row_groups = lax.axis_size("pairs")
    col_groups = lax.axis_size("chol")
    core_count = lax.axis_size("walk")
    core_index = lax.axis_index("walk")
    core_cols = slab_cols // core_count
    owner_count = row_groups * col_groups
    walker_total = owner_count * owner_walkers
    flat_vectors = chol_vectors.reshape(held_vectors, slab_rows * slab_cols)
    trial_split = trial_orbitals.reshape(col_groups, core_count, core_cols, electron_count)
    trial_part = lax.dynamic_index_in_dim(trial_split, core_index, 1, keepdims=False)
    walker_full = lax.all_gather(walkers, "walk", axis=2, tiled=True)
    outgoing = green_blocks(walker_full, trial_orbitals, trial_part, row_groups, col_groups)
    sectioned = outgoing.reshape(row_groups, col_groups, owner_walkers, slab_rows * core_cols)
    arrived = lax.all_to_all(
        lax.all_to_all(sectioned, "pairs", split_axis=0, concat_axis=0, tiled=True),
        "chol",
        split_axis=1,
        concat_axis=1,
        tiled=True,
    )
    arrived = arrived.reshape(walker_total, slab_rows, core_cols)
    partial_bias = jnp.einsum(
        "wab,gab->wg",
        lax.all_gather(arrived, "walk", axis=2, tiled=True),
        chol_vectors,
        preferred_element_type=jnp.float32,
    )
    force_bias = lax.psum(partial_bias, ("pairs", "chol"))
    bias_steps = [force_bias]
    shifted = field_noise[0] + root_step * force_bias
    shifted_high = lax.optimization_barrier(shifted.astype(jnp.bfloat16))
    shifted_low = (shifted - shifted_high.astype(jnp.float32)).astype(jnp.bfloat16)
    stacked = jnp.stack([shifted_high, shifted_low])
    both_parts = lax.dot_general(
        stacked, flat_vectors, (((2,), (0,)), ((), ())), preferred_element_type=jnp.float32
    )
    potential = both_parts[0] + both_parts[1]
    blocks_out = potential.reshape(owner_count, owner_walkers, slab_rows * slab_cols)
    received = lax.all_to_all(
        blocks_out, ("pairs", "chol"), split_axis=0, concat_axis=0, tiled=True
    )
    partner = swapped(received, "walk", 0)
    summed = (received + partner).reshape(
        row_groups, col_groups, owner_walkers, slab_rows, core_count, core_cols
    )
    matrix = jnp.transpose(summed, (2, 0, 3, 1, 4, 5)).reshape(
        owner_walkers, orbital_count, orbital_count
    )
    running_term = walkers
    running_sum = walkers
    for degree in range(1, TERMS):
        running_term = -(root_step / degree) * jnp.einsum(
            "wpq,wqm->wpm", matrix, running_term, precision=highest
        )
        running_sum = running_sum + running_term
    return (running_sum, jnp.stack(bias_steps))


PANEL = 32
TILE = 16
MIB = 2**20


def exact_dot(left, right, left_dim, right_dim):
    return lax.dot_general(
        left,
        right,
        (((left_dim,), (right_dim,)), ((), ())),
        precision=highest,
        preferred_element_type=jnp.float32,
    )


def fast_dot(left, right, left_dim, right_dim):
    return lax.dot_general(
        left, right, (((left_dim,), (right_dim,)), ((), ())), preferred_element_type=jnp.float32
    )


def green_kernel(row_groups, col_groups, walker_ref, trial_ref, out_ref, work):
    orbitals, electrons = walker_ref.shape
    core = lax.axis_index("walk")
    cores = lax.axis_size("walk")
    slab_rows = orbitals // row_groups
    slab_cols = orbitals // col_groups
    core_rows = slab_rows // cores
    half = core_rows // 2
    intersection = exact_dot(trial_ref[...], walker_ref[...], 0, 0)
    work[...] = exact_dot(intersection, intersection, 0, 0)
    lanes = lax.broadcasted_iota(jnp.int32, (PANEL, electrons), 1)
    rows = lax.broadcasted_iota(jnp.int32, (PANEL, electrons), 0)
    wide = lax.broadcasted_iota(jnp.int32, (electrons, electrons), 1)
    for start in range(0, electrons, PANEL):
        panel = work[start : start + PANEL, :]
        signed = jnp.where(lanes < start, -panel, panel)
        for step in range(0, PANEL, 2):
            lane = start + step
            left_col = panel[:, lane : lane + 1]
            right_col = panel[:, lane + 1 : lane + 2]
            a, b = left_col[step : step + 1], right_col[step : step + 1]
            c, d = left_col[step + 1 : step + 2], right_col[step + 1 : step + 2]
            scale = 1.0 / (a * d - b * c)
            pivots = (lanes == lane) | (lanes == lane + 1)
            unit_top = jnp.where(lanes[:1] == lane, 1.0, 0.0)
            unit_low = jnp.where(lanes[:1] == lane + 1, 1.0, 0.0)
            top = jnp.where(pivots[:1], unit_top, panel[step : step + 1, :])
            low = jnp.where(pivots[:1], unit_low, panel[step + 1 : step + 2, :])
            new_top = (d * scale) * top - (b * scale) * low
            new_low = (a * scale) * low - (c * scale) * top
            cleared = jnp.where(pivots, 0.0, panel) - left_col * new_top - right_col * new_low
            panel = jnp.where(rows == step, new_top, jnp.where(rows == step + 1, new_low, cleared))
        update = exact_dot(signed, panel, 0, 0)
        inside = (wide >= start) & (wide < start + PANEL)
        work[...] = jnp.where(inside, 0.0, work[...]) - update
        work[start : start + PANEL, :] = panel
    inverse = exact_dot(work[...], intersection, 1, 1)
    identity = jnp.where(
        lax.broadcasted_iota(jnp.int32, (electrons, electrons), 0) == wide, 1.0, 0.0
    )
    rest = identity - exact_dot(intersection, inverse, 1, 0)
    inverse = inverse + exact_dot(inverse, rest, 1, 0)
    chosen = jnp.concatenate(
        [
            walker_ref[pl.ds(pl.multiple_of(row * slab_rows + core * core_rows, 8), core_rows), :]
            for row in range(row_groups)
        ],
        axis=0,
    )
    left = exact_dot(chosen, inverse, 1, 0)
    for col in range(col_groups):
        block = exact_dot(left, trial_ref[col * slab_cols : (col + 1) * slab_cols, :], 1, 1)
        for row in range(row_groups):
            top = block[row * core_rows : row * core_rows + half]
            low = block[row * core_rows + half : (row + 1) * core_rows]
            out_ref[row * col_groups + col] = jnp.concatenate([top, low], axis=1).astype(jnp.bfloat16)


def walk_kernel(
    row_groups,
    col_groups,
    green_ref,
    vectors_ref,
    walker_ref,
    noise_ref,
    out_ref,
    bias_ref,
    held,
    greens,
    tiles,
    sums,
    first_sums,
    second_sums,
    partner,
    own,
    ready,
    arrived,
    matrix,
    load_sem,
    green_send,
    green_recv,
    pass_send,
    pass_recv,
    first_send,
    first_recv,
    second_send,
    second_recv,
    partner_send,
    partner_recv,
    out_send,
    out_recv,
    hand_send,
    hand_recv,
):
    owners = row_groups * col_groups
    slab_rows, slab_cols, window = held.shape
    half = green_ref.shape[1]
    pieces = half // TILE
    pair = lax.axis_index("pairs")
    place = lax.axis_index("chol")
    core = lax.axis_index("walk")
    me = pair * col_groups + place
    other = {"walk": 1 - core}

    def chip(index):
        return {"pairs": index // col_groups, "chol": index % col_groups}

    def to(shift):
        return lax.rem(me + shift, owners)

    def source(shift):
        return lax.rem(me + owners - shift, owners)

    def remote(src, dst, send, recv, target):
        return pltpu.make_async_remote_copy(
            src_ref=src,
            dst_ref=dst,
            send_sem=send,
            recv_sem=recv,
            device_id=target,
            device_id_type=pl.DeviceIdType.MESH,
        )

    parts = load_sem.shape[0]
    depth = slab_rows // parts
    loads = [
        pltpu.make_async_copy(
            vectors_ref.at[pl.ds(index * depth, depth)],
            held.at[pl.ds(index * depth, depth)],
            load_sem.at[index],
        )
        for index in range(parts)
    ]
    barrier = pltpu.get_barrier_semaphore()
    for shift in range(1, owners):
        pl.semaphore_signal(barrier, inc=1, device_id=chip(to(shift)), device_id_type=pl.DeviceIdType.MESH)
    pl.semaphore_signal(barrier, inc=1, device_id=other, device_id_type=pl.DeviceIdType.MESH)
    pl.semaphore_wait(barrier, owners)

    def green_copy(shift, slot):
        return remote(
            green_ref.at[to(shift)], greens.at[core, slot], green_send.at[shift],
            green_recv.at[shift], chip(to(shift)),
        )

    def pass_copy(shift, side):
        slot = source(shift)
        return remote(
            greens.at[side, slot], greens.at[side, slot], pass_send.at[shift], pass_recv.at[shift], other
        )

    for shift in range(1, owners):
        green_copy(shift, me).start()
    for load in loads:
        load.start()
    greens[core, me] = green_ref[me]
    pass_copy(0, core).start()
    for shift in range(1, owners):
        green_copy(shift, source(shift)).wait_recv()
        pass_copy(shift, core).start()
    for shift in range(1, owners):
        green_copy(shift, me).wait_send()
    for shift in range(owners):
        pass_copy(shift, 1 - core).wait_recv()
    for shift in range(owners):
        pass_copy(shift, core).wait_send()
    width = 2 * slab_cols
    for side in range(2):
        for piece in range(pieces):
            span = slice(piece * TILE, (piece + 1) * TILE)
            both = jnp.swapaxes(greens[side, :, span, :].astype(jnp.float32), 0, 1)
            row = side * 2 * half + piece * TILE
            tiles[row : row + TILE] = both[:, :, :slab_cols].astype(jnp.bfloat16)
            turned = pltpu.roll(both, slab_cols, 2)
            tiles[row + half : row + half + TILE] = turned[:, :, :slab_cols].astype(jnp.bfloat16)
    for load in loads:
        load.wait()

    sums[...] = jnp.zeros_like(sums)

    @pl.loop(0, slab_rows // TILE)
    def _(index):
        total = sums[...]
        for offset in range(TILE):
            row = index * TILE + offset
            total += fast_dot(tiles[row], held[row], 1, 0)
        sums[...] = total

    first_sums[place] = sums[...]

    def first_copy(shift, slot):
        target = lax.rem(place + shift, col_groups)
        return remote(
            first_sums.at[slot], first_sums.at[slot], first_send.at[shift], first_recv.at[shift], {"chol": target}
        )

    def second_copy(shift, slot):
        target = lax.rem(pair + shift, row_groups)
        return remote(
            second_sums.at[slot], second_sums.at[slot], second_send.at[shift], second_recv.at[shift], {"pairs": target}
        )

    for shift in range(1, col_groups):
        first_copy(shift, place).start()
    for shift in range(1, col_groups):
        first_copy(shift, lax.rem(place + col_groups - shift, col_groups)).wait_recv()
    summed = first_sums[0]
    for slot in range(1, col_groups):
        summed = summed + first_sums[slot]
    second_sums[pair] = summed
    for shift in range(1, row_groups):
        second_copy(shift, pair).start()
    for shift in range(1, row_groups):
        second_copy(shift, lax.rem(pair + row_groups - shift, row_groups)).wait_recv()
    bias = second_sums[0]
    for slot in range(1, row_groups):
        bias = bias + second_sums[slot]
    bias_ref[0] = bias
    for shift in range(1, col_groups):
        first_copy(shift, place).wait_send()
    for shift in range(1, row_groups):
        second_copy(shift, pair).wait_send()

    shifted = (noise_ref[0] + root_step * bias).astype(jnp.bfloat16)

    def potential(block):
        first = block * TILE
        lines = [fast_dot(shifted, held[first + offset], 1, 1) for offset in range(TILE)]
        return jnp.swapaxes(jnp.stack(lines), 0, 1)

    def packed(side, piece):
        first = side * 2 * pieces + piece
        return jnp.concatenate([potential(first), potential(first + pieces)], axis=2)

    def partner_copy(piece):
        return remote(
            own.at[piece], partner.at[piece], partner_send.at[piece], partner_recv.at[piece], other
        )

    def out_copy(piece, shift, slot):
        span = pl.ds(piece * TILE, TILE)
        return remote(
            ready.at[to(shift), span], arrived.at[core, slot, span], out_send.at[piece, shift],
            out_recv.at[piece, shift], chip(to(shift)),
        )

    def hand_copy(shift, side):
        slot = source(shift)
        return remote(
            arrived.at[side, slot], arrived.at[side, slot], hand_send.at[shift], hand_recv.at[shift], other
        )

    for piece in range(pieces):
        own[piece] = packed(1 - core, piece)
        partner_copy(piece).start()
    for piece in range(pieces):
        mine = packed(core, piece)
        partner_copy(piece).wait_recv()
        ready[:, piece * TILE : (piece + 1) * TILE, :] = (mine + partner[piece]).astype(jnp.bfloat16)
        for shift in range(1, owners):
            out_copy(piece, shift, me).start()
    arrived[core, me] = ready[me]
    hand_copy(0, core).start()
    for shift in range(1, owners):
        for piece in range(pieces):
            out_copy(piece, shift, source(shift)).wait_recv()
        hand_copy(shift, core).start()
    for piece in range(pieces):
        partner_copy(piece).wait_send()
        for shift in range(1, owners):
            out_copy(piece, shift, me).wait_send()
    for shift in range(owners):
        hand_copy(shift, 1 - core).wait_recv()
    for shift in range(owners):
        hand_copy(shift, core).wait_send()
    for slot in range(owners):
        for side in range(2):
            base = (slot // col_groups) * slab_rows + side * 2 * half
            both = arrived[side, slot]
            matrix[slot % col_groups, base : base + half, :] = both[:, :slab_cols]
            turned = pltpu.roll(both.astype(jnp.float32), slab_cols, 1)
            matrix[slot % col_groups, base + half : base + 2 * half, :] = turned[:, :slab_cols].astype(jnp.bfloat16)

    term = walker_ref[0]
    out_ref[0] = term
    share = term.shape[1]
    for degree in range(1, TERMS):
        high = term.astype(jnp.bfloat16)
        low = (term - high.astype(jnp.float32)).astype(jnp.bfloat16)
        sides = jnp.concatenate([high, low], axis=1)
        total = jnp.zeros((term.shape[0], 2 * share), jnp.float32)
        for col in range(col_groups):
            total += fast_dot(matrix[col], sides[col * slab_cols : (col + 1) * slab_cols], 1, 0)
        term = -(root_step / degree) * (total[:, :share] + total[:, share:])
        out_ref[0] = out_ref[0] + term


def fits(chol_vectors, trial_orbitals, walkers):
    window, slab_rows, slab_cols = chol_vectors.shape
    electrons = trial_orbitals.shape[1]
    owners = lax.axis_size("pairs") * lax.axis_size("chol")
    return (
        lax.axis_size("walk") == 2
        and walkers.shape[0] == 1
        and walkers.shape[1] == trial_orbitals.shape[0]
        and slab_rows % (4 * TILE) == 0
        and (2 * slab_cols) % 128 == 0
        and window % 128 == 0
        and electrons % 256 == 0
        and owners == TILE
        and chol_vectors.size <= 14 * MIB
    )


def shards(chol_vectors, trial_orbitals, walkers, field_noise):
    if field_noise.shape[0] != 1 or not fits(chol_vectors, trial_orbitals, walkers):
        return plain_shards(chol_vectors, trial_orbitals, walkers, field_noise)
    row_groups = lax.axis_size("pairs")
    col_groups = lax.axis_size("chol")
    owners = row_groups * col_groups
    window, slab_rows, slab_cols = chol_vectors.shape
    vectors_last = jnp.transpose(chol_vectors, (1, 2, 0))
    orbitals, electrons = trial_orbitals.shape
    half = slab_rows // 4
    width = 2 * slab_cols
    pieces = half // TILE
    walker_full = lax.all_gather(walkers[0], "walk", axis=1, tiled=True)
    in_vmem = pl.BlockSpec(memory_space=pltpu.VMEM)
    greens = pl.pallas_call(
        functools.partial(green_kernel, row_groups, col_groups),
        out_shape=jax.ShapeDtypeStruct((owners, half, width), jnp.bfloat16),
        in_specs=[in_vmem, in_vmem],
        out_specs=in_vmem,
        scratch_shapes=[pltpu.VMEM((electrons, electrons), jnp.float32)],
        compiler_params=pltpu.CompilerParams(vmem_limit_bytes=32 * MIB),
    )(walker_full, trial_orbitals)
    dma = pltpu.SemaphoreType.DMA
    propagated, bias = pl.pallas_call(
        functools.partial(walk_kernel, row_groups, col_groups),
        out_shape=(
            jax.ShapeDtypeStruct(walkers.shape, jnp.float32),
            jax.ShapeDtypeStruct(field_noise.shape, jnp.float32),
        ),
        in_specs=[in_vmem, pl.BlockSpec(memory_space=pl.ANY), in_vmem, in_vmem],
        out_specs=(in_vmem, in_vmem),
        scratch_shapes=[
            pltpu.VMEM(vectors_last.shape, jnp.bfloat16),
            pltpu.VMEM((2, owners, half, width), jnp.bfloat16),
            pltpu.VMEM((slab_rows, owners, slab_cols), jnp.bfloat16),
            pltpu.VMEM((owners, window), jnp.float32),
            pltpu.VMEM((col_groups, owners, window), jnp.float32),
            pltpu.VMEM((row_groups, owners, window), jnp.float32),
            pltpu.VMEM((pieces, owners, TILE, width), jnp.float32),
            pltpu.VMEM((pieces, owners, TILE, width), jnp.float32),
            pltpu.VMEM((owners, half, width), jnp.bfloat16),
            pltpu.VMEM((2, owners, half, width), jnp.bfloat16),
            pltpu.VMEM((col_groups, orbitals, slab_cols), jnp.bfloat16),
            dma((4,)),
            dma((owners,)),
            dma((owners,)),
            dma((owners,)),
            dma((owners,)),
            dma((col_groups,)),
            dma((col_groups,)),
            dma((row_groups,)),
            dma((row_groups,)),
            dma((pieces,)),
            dma((pieces,)),
            dma((pieces, owners)),
            dma((pieces, owners)),
            dma((owners,)),
            dma((owners,)),
        ],
        compiler_params=pltpu.CompilerParams(
            collective_id=0, has_side_effects=True, vmem_limit_bytes=56 * MIB
        ),
    )(greens, vectors_last, walkers, field_noise)
    return (propagated, bias)


def solution(mesh):
    placed = (
        P(("groups", "walk"), "pairs", "chol"),
        P("groups", None),
        P(("groups", "pairs", "chol"), None, "walk"),
        P("groups", None, "walk"),
    )
    return jax.shard_map(
        shards,
        mesh=mesh,
        in_specs=placed,
        out_specs=(P(("groups", "pairs", "chol"), None, "walk"), P("groups", None, "walk")),
        check_vma=False,
    )
```

```python
import functools

import jax
import jax.numpy as jnp
from jax import lax
from jax.experimental import pallas as pl
from jax.experimental.pallas import tpu as pltpu
from jax.sharding import PartitionSpec as P

TERMS = 6


root_step = 0.05
highest = lax.Precision.HIGHEST


def swapped(value, axis, apart):
    mask = 2**apart
    pairs = [(source, source ^ mask) for source in range(lax.axis_size(axis))]
    return lax.ppermute(value, axis, pairs)


def solve_normal(factor, right_side):
    middle = lax.linalg.triangular_solve(factor, right_side, left_side=True, lower=True)
    return lax.linalg.triangular_solve(factor, middle, left_side=True, lower=True, transpose_a=True)


def green_blocks(walker_full, trial_orbitals, trial_part, row_groups, col_groups):
    owner_walkers, orbital_count, electron_count = walker_full.shape
    intersection = jnp.einsum("nm,wnk->wmk", trial_orbitals, walker_full, precision=highest)
    normal = jnp.einsum("wmk,wml->wkl", intersection, intersection, precision=highest)
    factor = jnp.linalg.cholesky(normal)
    rotated = jnp.einsum("wmk,cbm->wkcb", intersection, trial_part, precision=highest)
    chosen_cols = rotated.shape[2] * rotated.shape[3]
    solved = solve_normal(factor, rotated.reshape(owner_walkers, electron_count, chosen_cols))
    slab_rows = orbital_count // row_groups
    block_cols = chosen_cols // col_groups
    shaped = solved.reshape(owner_walkers, electron_count, col_groups, block_cols)
    walker_rows = walker_full.reshape(owner_walkers, row_groups, slab_rows, electron_count)
    blocks = jnp.einsum("wiak,wkcb->icwab", walker_rows, shaped, precision=highest)
    return blocks.astype(jnp.bfloat16).reshape(
        row_groups * col_groups, owner_walkers, slab_rows * block_cols
    )


def plain_shards(chol_vectors, trial_orbitals, walkers, field_noise):
    held_vectors, slab_rows, slab_cols = chol_vectors.shape
    owner_walkers = walkers.shape[0]
    orbital_count = walkers.shape[1]
    electron_count = trial_orbitals.shape[1]
    row_groups = lax.axis_size("pairs")
    col_groups = lax.axis_size("chol")
    core_count = lax.axis_size("walk")
    core_index = lax.axis_index("walk")
    core_cols = slab_cols // core_count
    owner_count = row_groups * col_groups
    walker_total = owner_count * owner_walkers
    flat_vectors = chol_vectors.reshape(held_vectors, slab_rows * slab_cols)
    trial_split = trial_orbitals.reshape(col_groups, core_count, core_cols, electron_count)
    trial_part = lax.dynamic_index_in_dim(trial_split, core_index, 1, keepdims=False)
    walker_full = lax.all_gather(walkers, "walk", axis=2, tiled=True)
    outgoing = green_blocks(walker_full, trial_orbitals, trial_part, row_groups, col_groups)
    sectioned = outgoing.reshape(row_groups, col_groups, owner_walkers, slab_rows * core_cols)
    arrived = lax.all_to_all(
        lax.all_to_all(sectioned, "pairs", split_axis=0, concat_axis=0, tiled=True),
        "chol",
        split_axis=1,
        concat_axis=1,
        tiled=True,
    )
    arrived = arrived.reshape(walker_total, slab_rows, core_cols)
    partial_bias = jnp.einsum(
        "wab,gab->wg",
        lax.all_gather(arrived, "walk", axis=2, tiled=True),
        chol_vectors,
        preferred_element_type=jnp.float32,
    )
    force_bias = lax.psum(partial_bias, ("pairs", "chol"))
    bias_steps = [force_bias]
    shifted = field_noise[0] + root_step * force_bias
    shifted_high = lax.optimization_barrier(shifted.astype(jnp.bfloat16))
    shifted_low = (shifted - shifted_high.astype(jnp.float32)).astype(jnp.bfloat16)
    stacked = jnp.stack([shifted_high, shifted_low])
    both_parts = lax.dot_general(
        stacked, flat_vectors, (((2,), (0,)), ((), ())), preferred_element_type=jnp.float32
    )
    potential = both_parts[0] + both_parts[1]
    blocks_out = potential.reshape(owner_count, owner_walkers, slab_rows * slab_cols)
    received = lax.all_to_all(
        blocks_out, ("pairs", "chol"), split_axis=0, concat_axis=0, tiled=True
    )
    partner = swapped(received, "walk", 0)
    summed = (received + partner).reshape(
        row_groups, col_groups, owner_walkers, slab_rows, core_count, core_cols
    )
    matrix = jnp.transpose(summed, (2, 0, 3, 1, 4, 5)).reshape(
        owner_walkers, orbital_count, orbital_count
    )
    running_term = walkers
    running_sum = walkers
    for degree in range(1, TERMS):
        running_term = -(root_step / degree) * jnp.einsum(
            "wpq,wqm->wpm", matrix, running_term, precision=highest
        )
        running_sum = running_sum + running_term
    return (running_sum, jnp.stack(bias_steps))


PANEL = 32
TILE = 16
MIB = 2**20


def exact_dot(left, right, left_dim, right_dim):
    return lax.dot_general(
        left,
        right,
        (((left_dim,), (right_dim,)), ((), ())),
        precision=highest,
        preferred_element_type=jnp.float32,
    )


def fast_dot(left, right, left_dim, right_dim):
    return lax.dot_general(
        left, right, (((left_dim,), (right_dim,)), ((), ())), preferred_element_type=jnp.float32
    )


def green_kernel(row_groups, col_groups, walker_ref, trial_ref, out_ref, work):
    orbitals, electrons = walker_ref.shape
    core = lax.axis_index("walk")
    cores = lax.axis_size("walk")
    slab_rows = orbitals // row_groups
    slab_cols = orbitals // col_groups
    core_rows = slab_rows // cores
    half = core_rows // 2
    intersection = exact_dot(trial_ref[...], walker_ref[...], 0, 0)
    work[...] = exact_dot(intersection, intersection, 0, 0)
    lanes = lax.broadcasted_iota(jnp.int32, (PANEL, electrons), 1)
    rows = lax.broadcasted_iota(jnp.int32, (PANEL, electrons), 0)
    wide = lax.broadcasted_iota(jnp.int32, (electrons, electrons), 1)
    for start in range(0, electrons, PANEL):
        panel = work[start : start + PANEL, :]
        signed = jnp.where(lanes < start, -panel, panel)
        for step in range(PANEL):
            lane = start + step
            pivot_col = panel[:, lane : lane + 1]
            pivot = panel[step : step + 1, lane : lane + 1]
            scaled = jnp.where(lanes[:1] == lane, 1.0, panel[step : step + 1, :]) * (1.0 / pivot)
            cleared = jnp.where(lanes == lane, 0.0, panel) - pivot_col * scaled
            panel = jnp.where(rows == step, scaled, cleared)
        update = exact_dot(signed, panel, 0, 0)
        inside = (wide >= start) & (wide < start + PANEL)
        work[...] = jnp.where(inside, 0.0, work[...]) - update
        work[start : start + PANEL, :] = panel
    inverse = exact_dot(work[...], intersection, 1, 1)
    identity = jnp.where(
        lax.broadcasted_iota(jnp.int32, (electrons, electrons), 0) == wide, 1.0, 0.0
    )
    rest = identity - exact_dot(intersection, inverse, 1, 0)
    inverse = inverse + exact_dot(inverse, rest, 1, 0)
    chosen = jnp.concatenate(
        [
            walker_ref[pl.ds(pl.multiple_of(row * slab_rows + core * core_rows, 8), core_rows), :]
            for row in range(row_groups)
        ],
        axis=0,
    )
    left = exact_dot(chosen, inverse, 1, 0)
    for col in range(col_groups):
        block = exact_dot(left, trial_ref[col * slab_cols : (col + 1) * slab_cols, :], 1, 1)
        for row in range(row_groups):
            top = block[row * core_rows : row * core_rows + half]
            low = block[row * core_rows + half : (row + 1) * core_rows]
            out_ref[row * col_groups + col] = jnp.concatenate([top, low], axis=1).astype(jnp.bfloat16)


def walk_kernel(
    row_groups,
    col_groups,
    green_ref,
    vectors_ref,
    walker_ref,
    noise_ref,
    out_ref,
    bias_ref,
    held,
    greens,
    tiles,
    sums,
    first_sums,
    second_sums,
    partner,
    own,
    ready,
    arrived,
    matrix,
    load_sem,
    green_send,
    green_recv,
    pass_send,
    pass_recv,
    first_send,
    first_recv,
    second_send,
    second_recv,
    partner_send,
    partner_recv,
    out_send,
    out_recv,
    hand_send,
    hand_recv,
):
    owners = row_groups * col_groups
    slab_rows, slab_cols, window = held.shape
    half = green_ref.shape[1]
    pieces = half // TILE
    pair = lax.axis_index("pairs")
    place = lax.axis_index("chol")
    core = lax.axis_index("walk")
    me = pair * col_groups + place
    other = {"walk": 1 - core}

    def chip(index):
        return {"pairs": index // col_groups, "chol": index % col_groups}

    def to(shift):
        return lax.rem(me + shift, owners)

    def source(shift):
        return lax.rem(me + owners - shift, owners)

    def remote(src, dst, send, recv, target):
        return pltpu.make_async_remote_copy(
            src_ref=src,
            dst_ref=dst,
            send_sem=send,
            recv_sem=recv,
            device_id=target,
            device_id_type=pl.DeviceIdType.MESH,
        )

    parts = load_sem.shape[0]
    depth = slab_rows // parts
    loads = [
        pltpu.make_async_copy(
            vectors_ref.at[pl.ds(index * depth, depth)],
            held.at[pl.ds(index * depth, depth)],
            load_sem.at[index],
        )
        for index in range(parts)
    ]
    barrier = pltpu.get_barrier_semaphore()
    for shift in range(1, owners):
        pl.semaphore_signal(barrier, inc=1, device_id=chip(to(shift)), device_id_type=pl.DeviceIdType.MESH)
    pl.semaphore_signal(barrier, inc=1, device_id=other, device_id_type=pl.DeviceIdType.MESH)
    pl.semaphore_wait(barrier, owners)

    def green_copy(shift, slot):
        return remote(
            green_ref.at[to(shift)], greens.at[core, slot], green_send.at[shift],
            green_recv.at[shift], chip(to(shift)),
        )

    def pass_copy(shift, side):
        slot = source(shift)
        return remote(
            greens.at[side, slot], greens.at[side, slot], pass_send.at[shift], pass_recv.at[shift], other
        )

    for shift in range(1, owners):
        green_copy(shift, me).start()
    for load in loads:
        load.start()
    greens[core, me] = green_ref[me]
    pass_copy(0, core).start()
    for shift in range(1, owners):
        green_copy(shift, source(shift)).wait_recv()
        pass_copy(shift, core).start()
    for shift in range(1, owners):
        green_copy(shift, me).wait_send()
    for shift in range(owners):
        pass_copy(shift, 1 - core).wait_recv()
    for shift in range(owners):
        pass_copy(shift, core).wait_send()
    width = 2 * slab_cols
    for side in range(2):
        for piece in range(pieces):
            span = slice(piece * TILE, (piece + 1) * TILE)
            both = jnp.swapaxes(greens[side, :, span, :].astype(jnp.float32), 0, 1)
            row = side * 2 * half + piece * TILE
            tiles[row : row + TILE] = both[:, :, :slab_cols].astype(jnp.bfloat16)
            turned = pltpu.roll(both, slab_cols, 2)
            tiles[row + half : row + half + TILE] = turned[:, :, :slab_cols].astype(jnp.bfloat16)
    for load in loads:
        load.wait()

    sums[...] = jnp.zeros_like(sums)

    @pl.loop(0, slab_rows // TILE)
    def _(index):
        total = sums[...]
        for offset in range(TILE):
            row = index * TILE + offset
            total += fast_dot(tiles[row], held[row], 1, 0)
        sums[...] = total

    first_sums[place] = sums[...]

    def first_copy(shift, slot):
        target = lax.rem(place + shift, col_groups)
        return remote(
            first_sums.at[slot], first_sums.at[slot], first_send.at[shift], first_recv.at[shift], {"chol": target}
        )

    def second_copy(shift, slot):
        target = lax.rem(pair + shift, row_groups)
        return remote(
            second_sums.at[slot], second_sums.at[slot], second_send.at[shift], second_recv.at[shift], {"pairs": target}
        )

    for shift in range(1, col_groups):
        first_copy(shift, place).start()
    for shift in range(1, col_groups):
        first_copy(shift, lax.rem(place + col_groups - shift, col_groups)).wait_recv()
    summed = first_sums[0]
    for slot in range(1, col_groups):
        summed = summed + first_sums[slot]
    second_sums[pair] = summed
    for shift in range(1, row_groups):
        second_copy(shift, pair).start()
    for shift in range(1, row_groups):
        second_copy(shift, lax.rem(pair + row_groups - shift, row_groups)).wait_recv()
    bias = second_sums[0]
    for slot in range(1, row_groups):
        bias = bias + second_sums[slot]
    bias_ref[0] = bias
    for shift in range(1, col_groups):
        first_copy(shift, place).wait_send()
    for shift in range(1, row_groups):
        second_copy(shift, pair).wait_send()

    shifted = (noise_ref[0] + root_step * bias).astype(jnp.bfloat16)

    def potential(block):
        first = block * TILE
        lines = [fast_dot(shifted, held[first + offset], 1, 1) for offset in range(TILE)]
        return jnp.swapaxes(jnp.stack(lines), 0, 1)

    def packed(side, piece):
        first = side * 2 * pieces + piece
        return jnp.concatenate([potential(first), potential(first + pieces)], axis=2)

    def partner_copy(piece):
        return remote(
            own.at[piece], partner.at[piece], partner_send.at[piece], partner_recv.at[piece], other
        )

    def out_copy(piece, shift, slot):
        span = pl.ds(piece * TILE, TILE)
        return remote(
            ready.at[to(shift), span], arrived.at[core, slot, span], out_send.at[piece, shift],
            out_recv.at[piece, shift], chip(to(shift)),
        )

    def hand_copy(shift, side):
        slot = source(shift)
        return remote(
            arrived.at[side, slot], arrived.at[side, slot], hand_send.at[shift], hand_recv.at[shift], other
        )

    for piece in range(pieces):
        own[piece] = packed(1 - core, piece)
        partner_copy(piece).start()
    for piece in range(pieces):
        mine = packed(core, piece)
        partner_copy(piece).wait_recv()
        ready[:, piece * TILE : (piece + 1) * TILE, :] = (mine + partner[piece]).astype(jnp.bfloat16)
        for shift in range(1, owners):
            out_copy(piece, shift, me).start()
    arrived[core, me] = ready[me]
    hand_copy(0, core).start()
    for shift in range(1, owners):
        for piece in range(pieces):
            out_copy(piece, shift, source(shift)).wait_recv()
        hand_copy(shift, core).start()
    for piece in range(pieces):
        partner_copy(piece).wait_send()
        for shift in range(1, owners):
            out_copy(piece, shift, me).wait_send()
    for shift in range(owners):
        hand_copy(shift, 1 - core).wait_recv()
    for shift in range(owners):
        hand_copy(shift, core).wait_send()
    for slot in range(owners):
        for side in range(2):
            base = (slot // col_groups) * slab_rows + side * 2 * half
            both = arrived[side, slot]
            matrix[slot % col_groups, base : base + half, :] = both[:, :slab_cols]
            turned = pltpu.roll(both.astype(jnp.float32), slab_cols, 1)
            matrix[slot % col_groups, base + half : base + 2 * half, :] = turned[:, :slab_cols].astype(jnp.bfloat16)

    term = walker_ref[0]
    out_ref[0] = term
    share = term.shape[1]
    for degree in range(1, TERMS):
        high = term.astype(jnp.bfloat16)
        low = (term - high.astype(jnp.float32)).astype(jnp.bfloat16)
        sides = jnp.concatenate([high, low], axis=1)
        total = jnp.zeros((term.shape[0], 2 * share), jnp.float32)
        for col in range(col_groups):
            total += fast_dot(matrix[col], sides[col * slab_cols : (col + 1) * slab_cols], 1, 0)
        term = -(root_step / degree) * (total[:, :share] + total[:, share:])
        out_ref[0] = out_ref[0] + term


def fits(chol_vectors, trial_orbitals, walkers):
    window, slab_rows, slab_cols = chol_vectors.shape
    electrons = trial_orbitals.shape[1]
    owners = lax.axis_size("pairs") * lax.axis_size("chol")
    return (
        lax.axis_size("walk") == 2
        and walkers.shape[0] == 1
        and walkers.shape[1] == trial_orbitals.shape[0]
        and slab_rows % (4 * TILE) == 0
        and (2 * slab_cols) % 128 == 0
        and window % 128 == 0
        and electrons % 256 == 0
        and owners == TILE
        and chol_vectors.size <= 14 * MIB
    )


def shards(chol_vectors, trial_orbitals, walkers, field_noise):
    if field_noise.shape[0] != 1 or not fits(chol_vectors, trial_orbitals, walkers):
        return plain_shards(chol_vectors, trial_orbitals, walkers, field_noise)
    row_groups = lax.axis_size("pairs")
    col_groups = lax.axis_size("chol")
    owners = row_groups * col_groups
    window, slab_rows, slab_cols = chol_vectors.shape
    vectors_last = jnp.transpose(chol_vectors, (1, 2, 0))
    orbitals, electrons = trial_orbitals.shape
    half = slab_rows // 4
    width = 2 * slab_cols
    pieces = half // TILE
    walker_full = lax.all_gather(walkers[0], "walk", axis=1, tiled=True)
    in_vmem = pl.BlockSpec(memory_space=pltpu.VMEM)
    greens = pl.pallas_call(
        functools.partial(green_kernel, row_groups, col_groups),
        out_shape=jax.ShapeDtypeStruct((owners, half, width), jnp.bfloat16),
        in_specs=[in_vmem, in_vmem],
        out_specs=in_vmem,
        scratch_shapes=[pltpu.VMEM((electrons, electrons), jnp.float32)],
        compiler_params=pltpu.CompilerParams(vmem_limit_bytes=32 * MIB),
    )(walker_full, trial_orbitals)
    dma = pltpu.SemaphoreType.DMA
    propagated, bias = pl.pallas_call(
        functools.partial(walk_kernel, row_groups, col_groups),
        out_shape=(
            jax.ShapeDtypeStruct(walkers.shape, jnp.float32),
            jax.ShapeDtypeStruct(field_noise.shape, jnp.float32),
        ),
        in_specs=[in_vmem, pl.BlockSpec(memory_space=pl.ANY), in_vmem, in_vmem],
        out_specs=(in_vmem, in_vmem),
        scratch_shapes=[
            pltpu.VMEM(vectors_last.shape, jnp.bfloat16),
            pltpu.VMEM((2, owners, half, width), jnp.bfloat16),
            pltpu.VMEM((slab_rows, owners, slab_cols), jnp.bfloat16),
            pltpu.VMEM((owners, window), jnp.float32),
            pltpu.VMEM((col_groups, owners, window), jnp.float32),
            pltpu.VMEM((row_groups, owners, window), jnp.float32),
            pltpu.VMEM((pieces, owners, TILE, width), jnp.float32),
            pltpu.VMEM((pieces, owners, TILE, width), jnp.float32),
            pltpu.VMEM((owners, half, width), jnp.bfloat16),
            pltpu.VMEM((2, owners, half, width), jnp.bfloat16),
            pltpu.VMEM((col_groups, orbitals, slab_cols), jnp.bfloat16),
            dma((4,)),
            dma((owners,)),
            dma((owners,)),
            dma((owners,)),
            dma((owners,)),
            dma((col_groups,)),
            dma((col_groups,)),
            dma((row_groups,)),
            dma((row_groups,)),
            dma((pieces,)),
            dma((pieces,)),
            dma((pieces, owners)),
            dma((pieces, owners)),
            dma((owners,)),
            dma((owners,)),
        ],
        compiler_params=pltpu.CompilerParams(
            collective_id=0, has_side_effects=True, vmem_limit_bytes=56 * MIB
        ),
    )(greens, vectors_last, walkers, field_noise)
    return (propagated, bias)


def solution(mesh):
    placed = (
        P(("groups", "walk"), "pairs", "chol"),
        P("groups", None),
        P(("groups", "pairs", "chol"), None, "walk"),
        P("groups", None, "walk"),
    )
    return jax.shard_map(
        shards,
        mesh=mesh,
        in_specs=placed,
        out_specs=(P(("groups", "pairs", "chol"), None, "walk"), P("groups", None, "walk")),
        check_vma=False,
    )
```
